256 devices in a mesh: virt: 32 (over z, x_hi, core), aux: 8 (over x_lo, y).
Axes of the slice: x: 4 (x_hi: 2, x_lo: 2; x = x_hi * 2 + x_lo), y: 4, z: 8, core: 2. Of those that a mesh axis runs over, the one named last changes fastest.
Arguments:
- factors: bfloat16 [1920, 640, 640], P('aux', 'virt'), may hold values from -0.8984375 to 0.8984375
- lambda_pairs: bfloat16 [2, 640, 640], P(None, 'aux'), may hold values from -0.009765625 to 0.009765625
Outputs:
- ladder: float32 [2, 640, 3, 20], P(None, 'virt')
The draws below stay inside these ranges and needn't reach their ends.
All inputs are finite; a program needn't handle non-finite values.
Results may differ from the reference program's by a relative error of at most 0.0027.
Values may be sent and summed in bfloat16 or wider, within the bound.
No kernel may reach another device: no remote copies, remote signals or barrier semaphores. Data moves between devices by JAX's collectives and lax.ppermute only.
A program may use at most 128 MiB of HBM per device.

```python
import jax
import jax.numpy as jnp
from jax import lax

V = 640
NAUX = 1920
NPAIR = 2
N_VIRT = 32


def steps_of(rng, extent, pieces, low, high):
    level = 1.0
    for axis_at, blocks in pieces:
        steps = jax.random.uniform(jax.random.fold_in(jax.random.fold_in(rng, 6), axis_at), (blocks,), jnp.float32, low / len(pieces), high / len(pieces))
        level = level * jnp.repeat(jnp.exp(steps), extent[axis_at] // blocks).reshape((-1,) + (1,) * (len(extent) - 1 - axis_at))
    return level


def normal_values(key, dims, deviation, limit, shards=(), kind=jnp.bfloat16):
    array = deviation * jax.random.normal(key, dims, jnp.float32)
    if shards:
        array = array * steps_of(key, dims, shards, -0.22, 0.18)
    return jnp.clip(array, -limit, limit).astype(kind)


def setup_inputs(seed: int = 0) -> dict:
    streams_of = jax.random.split(jax.random.key(seed), 3)
    factors = normal_values(streams_of[0], (NAUX, V, V), 0.15, 0.8984375, ((0, 8), (1, 32)))
    lambda_pairs = normal_values(streams_of[1], (NPAIR, V, V), (V * V) ** -0.5, 0.009765625, ((1, 8),))
    return {"factors": factors, "lambda_pairs": lambda_pairs}


def reference(factors, lambda_pairs):
    block_width = V // N_VIRT
    lambda_wide = lambda_pairs.astype(jnp.float32)

    def one_block(index):
        start = (index * block_width).astype(jnp.int32)
        rows = lax.dynamic_slice_in_dim(factors, start, block_width, 1).astype(jnp.float32)
        contracted = jnp.einsum("pbd,ncd->npbc", rows, lambda_wide)
        contracted = lax.optimization_barrier(contracted.astype(jnp.bfloat16)).astype(jnp.float32)
        tiles = []
        for offset in range(3):
            owner = ((index - offset + 1) % N_VIRT).astype(jnp.int32)
            own_rows = lax.dynamic_slice_in_dim(factors, (owner * block_width).astype(jnp.int32), block_width, 1)
            tiles.append(jnp.einsum("pac,npbc->nab", own_rows.astype(jnp.float32), contracted))
        return jnp.stack(tiles, 0)

    results = lax.map(one_block, jnp.arange(N_VIRT, dtype=jnp.int32))
    shifted = [jnp.roll(results[:, offset], 1 - offset, axis=0) for offset in range(3)]
    whole = jnp.stack(shifted, 1)
    return whole.transpose(2, 0, 3, 1, 4).reshape(NPAIR, V, 3, block_width)
```

```python
import jax
import jax.numpy as jnp
from jax import lax
from jax.sharding import PartitionSpec as P

AXES = ("virt", "aux")
BLOCK = 16
FAR_CHUNKS = (64, 48)


def index_of(x, y, z, core):
    return ((z % 8 * 2 + x % 4 // 2) * 2 + core) * 8 + x % 2 * 4 + y % 4


def place_of(index):
    virt, aux = divmod(index, 8)
    return virt // 2 % 2 * 2 + aux // 4, aux % 4, virt // 4, virt % 2


def route(target, chosen=lambda core: True):
    places = [(i, place_of(i)) for i in range(256)]
    return [(i, index_of(*target(*p))) for i, p in places if chosen(p[3])]


def other_core(x, y, z, core):
    return x, y, z, 1 - core


def across(x, y, z, core):
    step = 1 if core else -1
    chip = z * 2 + x // 2 + step
    return chip % 2 * 2 + x % 2, y, chip // 2 % 8, 1 - core


NEAR, FAR = route(other_core), route(across)


def send(array, pairs):
    return lax.ppermute(array, AXES, pairs)


def gather_lambda(own, core, x_lo, y_at):
    half = lax.dynamic_index_in_dim(own, core, 0, keepdims=False)
    beside = send(half, route(lambda x, y, z, c: (x ^ (3 if c else 1), y, z, c)))
    both = jnp.where(x_lo == 0, jnp.stack([half, beside]), jnp.stack([beside, half]))
    parts = [both] + [
        send(both, route(lambda x, y, z, c, k=k: (x, y - k, z, c))) for k in (1, 2, 3)
    ]
    ring = jnp.stack(parts * 2, 1)
    mine = lax.dynamic_slice_in_dim(ring, (4 - y_at) % 4, 4, 1).reshape(640, 640)
    theirs = send(mine, NEAR)
    return jnp.where(core == 0, jnp.stack([mine, theirs]), jnp.stack([theirs, mine]))


def body(factors, lambda_pairs):
    virt, aux = lax.axis_index("virt"), lax.axis_index("aux")
    core, x_lo, y_at = virt % 2, aux // 4, aux % 4
    own = factors.transpose(1, 0, 2)
    kept = lax.dynamic_slice_in_dim(own, core * 112, 128, 1)
    sent = lax.dynamic_slice_in_dim(own, (1 - core) * 112, 112, 1)
    last = own[:, 224:]
    even_only = lambda pairs: [(s, t) for s, t in pairs if s // 8 % 2 == 0]

    pieces, at = [], 0
    for size in FAR_CHUNKS:
        pieces.append(send(sent[:, at : at + size], FAR))
        at += size
    pieces.append(send(last, even_only(FAR)))
    near = [send(sent, NEAR), send(last, even_only(NEAR))]

    lam = gather_lambda(lambda_pairs, core, x_lo, y_at)
    z_own = jnp.einsum("bpd,ncd->nbpc", own, lam, preferred_element_type=jnp.float32).astype(jnp.bfloat16)
    x_own = jnp.einsum("apc,ncd->napd", kept, lam, preferred_element_type=jnp.float32).astype(jnp.bfloat16)
    z_kept = lax.dynamic_slice_in_dim(z_own, core * 112, 128, 2)

    def dots(left, right):
        return jnp.einsum("napc,bpc->nab", left, right, preferred_element_type=jnp.float32)

    def edge(blocks):
        here, there, at = 0.0, 0.0, 0
        for b in blocks:
            stop = at + b.shape[1]
            here = here + dots(x_own[:, :, at:stop], b)
            there = there + dots(z_kept[:, :, at:stop], b)
            at = stop
        return here, there.transpose(0, 2, 1)

    diag = dots(z_own, own).transpose(0, 2, 1)
    near_here, near_there = edge(near)
    far_here, far_there = edge(pieces)
    near_all = near_here + send(near_there, NEAR)
    far_all = far_here + send(far_there, FAR)
    before = jnp.where(core == 0, far_all, near_all)
    after = jnp.where(core == 0, near_all, far_all)
    total = jnp.stack([before, diag, after], 2).reshape(20, 120)
    for k in (4, 1, 2):
        total = total + lax.ppermute(total, "aux", [(a, a ^ k) for a in range(8)])
    return total.reshape(2, 20, 3, 20)


def solution(mesh):
    placed = (P("aux", "virt", None), P(None, "aux", None))
    return jax.shard_map(
        body, mesh=mesh, in_specs=placed, out_specs=P(None, "virt", None, None), check_vma=False
    )
```

```python
import functools

import jax
import jax.numpy as jnp
from jax import lax
from jax.experimental import pallas as pl
from jax.experimental.pallas import tpu as pltpu
from jax.sharding import PartitionSpec as P

AXES = ("virt", "aux")
ROWS = 16
GROUP = 4
STEPS = 4
KEPT = 8
FREE = pl.CostEstimate(flops=1, bytes_accessed=1, transcendentals=0)
NT = (((1,), (1,)), ((), ()))
NN = (((1,), (0,)), ((), ()))


def index_of(x, y, z, core):
    return ((z % 8 * 2 + x % 4 // 2) * 2 + core) * 8 + x % 2 * 4 + y % 4


def place_of(index):
    virt, aux = divmod(index, 8)
    return virt // 2 % 2 * 2 + aux // 4, aux % 4, virt // 4, virt % 2


def route(target):
    return [(i, index_of(*target(*place_of(i)))) for i in range(256)]


def from_even(pairs):
    return [(s, t) for s, t in pairs if s // 8 % 2 == 0]


def other_core(x, y, z, core):
    return x, y, z, 1 - core


def across(x, y, z, core):
    step = 1 if core else -1
    chip = z * 2 + x // 2 + step
    return chip % 2 * 2 + x % 2, y, chip // 2 % 8, 1 - core


NEAR, FAR = route(other_core), route(across)


def send(array, pairs):
    return lax.ppermute(array, AXES, pairs)


def beside_lambda(own, core):
    half = lax.dynamic_index_in_dim(own, core, 0, keepdims=False)
    return half, send(half, route(lambda x, y, z, c: (x ^ (3 if c else 1), y, z, c)))


def gather_lambda(half, beside):
    both = jnp.stack([half, beside])

    def from_y(array, step):
        return send(array, route(lambda x, y, z, c: (x, y - step, z, c)))

    up, down = from_y(both, 1), from_y(both, -1)
    both, up, down = lax.optimization_barrier((both, up, down))
    mine = jnp.concatenate([both, up, from_y(both, 2), down])
    return mine, send(mine, NEAR)


def in_order(tile, core):
    half = tile.shape[1] // 2
    return jnp.where(core == 0, tile, jnp.concatenate([tile[:, half:], tile[:, :half]], 1))


def dot(left, right, dims):
    return lax.dot_general(left, right, dims, preferred_element_type=jnp.float32)


def folded(total, columns):
    wide = columns * ROWS
    row = lax.broadcasted_iota(jnp.int32, (ROWS, wide), 0)
    column = lax.broadcasted_iota(jnp.int32, (ROWS, wide), 1) % ROWS
    kept = jnp.where((row == column)[None], total.reshape(-1, ROWS, wide), 0.0).sum(1)
    group = lax.broadcasted_iota(jnp.int32, (wide, columns), 0) // ROWS
    ones = (group == lax.broadcasted_iota(jnp.int32, (wide, columns), 1)).astype(jnp.float32)
    return lax.dot_general(
        kept, ones, NN, precision=lax.Precision.HIGHEST, preferred_element_type=jnp.float32
    )


def side_by_side(parts):
    return jnp.concatenate(parts, 1)


def block(array, g):
    return array[:, g * ROWS : (g + 1) * ROWS].reshape(320, -1)


def own_kernel(
    place_ref, f_ref, mine_ref, theirs_ref, near_ref, sides_ref, diag_ref, near_tile_ref,
    diag, tile, lam, turned,
):
    step, core = pl.program_id(0), place_ref[0]

    @pl.when(step == 0)
    def _():
        diag[...] = jnp.zeros_like(diag)
        tile[...] = jnp.zeros_like(tile)
        for k in range(8):
            x_lo, y_at = (place_ref[1] + k % 2) % 2, (place_ref[2] + k // 2) % 4
            at = pl.ds(pl.multiple_of((x_lo * 4 + y_at) * 80, ROWS), 80)
            lam[0, at] = mine_ref[k]
            lam[1, at] = theirs_ref[k]
        for n in range(2):
            turned[:, n * 640 : (n + 1) * 640] = lam[n].T

    others = 8 * (1 - core) + jnp.where(step == 2, 0, 3)
    first = jnp.where(step < 2, 7 * core + 4 * step, others)
    at = pl.ds(pl.multiple_of(first * ROWS, ROWS), GROUP * ROWS)
    group = f_ref[:, at, :]
    rows = group.reshape(20 * GROUP * ROWS, 640)
    z = dot(rows, turned[...], NN).astype(jnp.bfloat16).reshape(20, GROUP * ROWS, 1280)

    def z_block(g):
        both = block(z, g)
        return jnp.concatenate([both[:, :640], both[:, 640:]], 0)

    z_blocks = [z_block(g) for g in range(GROUP)]
    own = [block(group, g) for g in range(GROUP)]
    own[0] = jnp.where(step == 3, jnp.zeros_like(own[0]), own[0])
    diag[...] += dot(side_by_side(own), side_by_side(z_blocks), NT)

    @pl.when(step < 2)
    def _():
        for n in range(2):
            x = dot(rows, lam[n], NN).astype(jnp.bfloat16).reshape(20, GROUP * ROWS, 640)
            for g in range(GROUP):
                sides_ref[g, n] = block(x, g)
        for g in range(GROUP):
            sides_ref[g, 2:] = z_blocks[g].reshape(2, 320, 640)
        near = near_ref[:, at, :]
        there = [block(near, g) for g in range(GROUP)]
        shared = jnp.logical_and(step == 1, core == 0)
        there[-1] = jnp.where(shared, jnp.zeros_like(there[-1]), there[-1])
        here = side_by_side([sides_ref[g].reshape(1280, 640) for g in range(GROUP)])
        tile[...] += dot(side_by_side(there), here, NT)

    @pl.when(step == STEPS - 1)
    def _():
        diag_ref[...] = folded(diag[...], 40)
        near_tile_ref[...] = folded(tile[...], 80)


def own_part(place, own, mine, theirs, near):
    whole = pl.BlockSpec(memory_space=pltpu.VMEM)
    return pl.pallas_call(
        own_kernel,
        grid_spec=pltpu.PrefetchScalarGridSpec(
            num_scalar_prefetch=1,
            grid=(STEPS,),
            in_specs=[whole] * 4,
            out_specs=[
                pl.BlockSpec((GROUP, 4, 320, 640), lambda g, c: (jnp.minimum(g, 1), 0, 0, 0)),
                pl.BlockSpec((20, 40), lambda g, c: (0, 0)),
                pl.BlockSpec((20, 80), lambda g, c: (0, 0)),
            ],
            scratch_shapes=[
                pltpu.VMEM((320, 640), jnp.float32),
                pltpu.VMEM((320, 1280), jnp.float32),
                pltpu.VMEM((2, 640, 640), jnp.bfloat16),
                pltpu.VMEM((640, 1280), jnp.bfloat16),
            ],
        ),
        out_shape=[
            jax.ShapeDtypeStruct((KEPT, 4, 320, 640), jnp.bfloat16),
            jax.ShapeDtypeStruct((20, 40), jnp.float32),
            jax.ShapeDtypeStruct((20, 80), jnp.float32),
        ],
        compiler_params=pltpu.CompilerParams(vmem_limit_bytes=60 << 20),
        cost_estimate=FREE,
        name="own_part",
    )(place, own, mine, theirs, near)


def edge_kernel(groups, *refs):
    *there_refs, tile_ref = refs
    there_refs, side_refs = there_refs[: -sum(groups)], there_refs[-sum(groups) :]
    there = [block(r, g) for r in there_refs for g in range(r.shape[1] // ROWS)]
    total, at = 0.0, 0
    for size in groups:
        here = side_by_side([r[0].reshape(1280, 640) for r in side_refs[at : at + size]])
        total = total + dot(side_by_side(there[at : at + size]), here, NT)
        at += size
    tile_ref[...] = folded(total, 80)


def edge_part(there, sides, blocks, groups):
    def side(k):
        return pl.BlockSpec((1, 4, 320, 640), lambda g: (k, 0, 0, 0))

    return pl.pallas_call(
        functools.partial(edge_kernel, groups),
        grid=(1,),
        in_specs=[pl.BlockSpec(t.shape, lambda g: (0, 0, 0)) for t in there] + [side(k) for k in blocks],
        out_specs=pl.BlockSpec((20, 80), lambda g: (0, 0)),
        out_shape=jax.ShapeDtypeStruct((20, 80), jnp.float32),
        compiler_params=pltpu.CompilerParams(vmem_limit_bytes=60 << 20),
        cost_estimate=FREE,
        name="edge_part",
    )(*there, *[sides] * len(blocks))


def flipped(tile):
    return tile.reshape(20, 2, 20).transpose(2, 1, 0).reshape(20, 40)


def body(factors, lambda_pairs):
    virt, aux = lax.axis_index("virt"), lax.axis_index("aux")
    core, x_lo, y_at = virt % 2, aux // 4, aux % 4
    own = factors.transpose(1, 0, 2)
    near = send(own, NEAR)
    half, beside = beside_lambda(lambda_pairs, core)

    def part(first, blocks):
        return lax.dynamic_slice_in_dim(own, ((1 - core) * 7 + first) * ROWS, blocks * ROWS, 1)

    last, most, rest = own[:, 14 * ROWS :], part(0, 5), part(5, 2)
    beside, last, most, rest = lax.optimization_barrier((beside, last, most, rest))
    last, most, rest = send(last, from_even(FAR)), send(most, FAR), send(rest, FAR)

    def before_far(own, near, half, beside):
        mine, theirs = gather_lambda(half, beside)
        place = jnp.stack([core, x_lo, y_at]).astype(jnp.int32)
        sides, diag, tile = own_part(place, own, mine, theirs, near)
        here, there = in_order(flipped(tile[:, :40]), core), in_order(tile[:, 40:], core)
        return sides, jnp.concatenate([in_order(diag, core), here + send(there, NEAR)], 1)

    sides, done = early(before_far, virt, own, near, half, beside)

    tile = edge_part([most, last], sides, (0, 1, 2, 3, 4, 7), (3, 3))
    tile = tile + edge_part([rest], sides, (5, 6), (2,))
    here = jnp.concatenate([in_order(flipped(tile[:, :40]), core), done], 1)
    there = in_order(tile[:, 40:], core)
    beside = lambda pairs: [(s, t ^ 4) for s, t in pairs]
    from_far = send(there, FAR) + send(there, beside(FAR))
    total = here + send(here, beside([(i, i) for i in range(256)]))
    total = total + jnp.pad(from_far, ((0, 0), (0, 80)))
    total = total + sum(lax.ppermute(total, "aux", [(a, a ^ k) for a in range(8)]) for k in (1, 2, 3))
    far_tile, diag, near_tile = [total[:, i * 40 : i * 40 + 40].reshape(20, 2, 20) for i in range(3)]
    before = jnp.where(core == 0, far_tile, near_tile)
    after = jnp.where(core == 0, near_tile, far_tile)
    return jnp.stack([before, diag, after], 2).transpose(1, 0, 2, 3)


def early(part, virt, *operands):
    def nothing(*operands):
        shapes = jax.eval_shape(part, *operands)
        return jax.tree.map(lambda s: jnp.zeros(s.shape, s.dtype), shapes)

    return lax.cond(virt < lax.axis_size("virt"), part, nothing, *operands)


def solution(mesh):
    placed = (P("aux", "virt", None), P(None, "aux", None))
    return jax.shard_map(
        body, mesh=mesh, in_specs=placed, out_specs=P(None, "virt", None, None), check_vma=False
    )
```

```python
import functools

import jax
import jax.numpy as jnp
from jax import lax
from jax.experimental import pallas as pl
from jax.experimental.pallas import tpu as pltpu
from jax.sharding import PartitionSpec as P

AXES = ("virt", "aux")
ROWS = 16
KEPT = 8
FREE = pl.CostEstimate(flops=1, bytes_accessed=1, transcendentals=0)
NT = (((1,), (1,)), ((), ()))
NN = (((1,), (0,)), ((), ()))


def index_of(x, y, z, core):
    return ((z % 8 * 2 + x % 4 // 2) * 2 + core) * 8 + x % 2 * 4 + y % 4


def place_of(index):
    virt, aux = divmod(index, 8)
    return virt // 2 % 2 * 2 + aux // 4, aux % 4, virt // 4, virt % 2


def route(target):
    return [(i, index_of(*target(*place_of(i)))) for i in range(256)]


def from_even(pairs):
    return [(s, t) for s, t in pairs if s // 8 % 2 == 0]


def other_core(x, y, z, core):
    return x, y, z, 1 - core


def across(x, y, z, core):
    step = 1 if core else -1
    chip = z * 2 + x // 2 + step
    return chip % 2 * 2 + x % 2, y, chip // 2 % 8, 1 - core


NEAR, FAR, HERE = route(other_core), route(across), [(i, i) for i in range(256)]


def send(array, pairs):
    return lax.ppermute(array, AXES, pairs)


def beside_lambda(own, core):
    half = lax.dynamic_index_in_dim(own, core, 0, keepdims=False)
    return half, send(half, route(lambda x, y, z, c: (x ^ (3 if c else 1), y, z, c)))


def dot(left, right, dims):
    return lax.dot_general(left, right, dims, preferred_element_type=jnp.float32)


def folded(total, core):
    wide = total.shape[1]
    columns = wide // ROWS
    row = lax.broadcasted_iota(jnp.int32, (ROWS, wide), 0)
    column = lax.broadcasted_iota(jnp.int32, (ROWS, wide), 1) % ROWS
    kept = jnp.where((row == column)[None], total.reshape(-1, ROWS, wide), 0.0).sum(1)
    group = lax.broadcasted_iota(jnp.int32, (wide, columns), 0) // ROWS
    place = group // 40 * 40 + (group + 20 * core) % 40
    ones = (place == lax.broadcasted_iota(jnp.int32, (wide, columns), 1)).astype(jnp.float32)
    return lax.dot_general(
        kept, ones, NN, precision=lax.Precision.HIGHEST, preferred_element_type=jnp.float32
    )


def side_by_side(parts):
    return jnp.concatenate(parts, 1)


def block(array, g):
    return array[:, g * ROWS : (g + 1) * ROWS].reshape(320, -1)


def own_kernel(
    place_ref, f_hbm, *refs
):
    lam_refs, (sides_hbm, diag_ref, f_buf, sides, rows_cd, cols_cd, f_sem, sides_sem) = refs[:8], refs[8:]
    core = place_ref[0]
    firsts = (7 * core, 7 * core + 4, 8 * (1 - core), 8 * (1 - core) + 4)
    sizes = (4, 4, 4, 3)

    def copied(step):
        count = sizes[step] * ROWS
        rows = pl.ds(pl.multiple_of(firsts[step] * ROWS, ROWS), count)
        return pltpu.make_async_copy(
            f_hbm.at[:, rows, :], f_buf.at[step, :, pl.ds(0, count), :], f_sem.at[step]
        )

    f_copies = [copied(step) for step in range(4)]
    side_copies = [
        pltpu.make_async_copy(sides.at[pair], sides_hbm.at[pair], sides_sem.at[pair]) for pair in range(4)
    ]
    for copy in f_copies:
        copy.start()

    for k in range(8):
        x_lo, y_at = place_ref[1] ^ (k % 2), (place_ref[2] + k // 2) % 4
        at = pl.ds(pl.multiple_of((x_lo * 4 + y_at) * 80, ROWS), 80)
        for n in range(2):
            part = lam_refs[4 * n + k // 2][k % 2]
            rows_cd[n, at] = part
            cols_cd[at, 640 * n : 640 * n + 640] = part

    diag = 0.0
    for step, size in enumerate(sizes):
        f_copies[step].wait()
        group = f_buf[step, :, : size * ROWS]
        rows = group.reshape(20 * size * ROWS, 640)
        first = 2 * min(step, 2)

        def keep(product, q):
            product = product.astype(jnp.bfloat16).reshape(20, size * ROWS, 1280)
            for n in range(2):
                for g in range(size):
                    part = product[:, g * ROWS : (g + 1) * ROWS, 640 * n : 640 * n + 640].reshape(320, 640)
                    at = (first + g // 2, slice(320 * (q + n), 320 * (q + n) + 320), pl.ds(640 * (g % 2), 640))
                    sides[at] = part

        keep(dot(rows, rows_cd[...].reshape(1280, 640), NT), 2)
        if step < 2:
            keep(dot(rows, cols_cd[...], NN), 0)
            for copy in side_copies[first : first + 2]:
                copy.start()
        for g in range(0, size, 2):
            count = min(2, size - g)
            own = side_by_side([block(group, g + k) for k in range(count)])
            diag = diag + dot(own, sides[first + g // 2, 640:, : 640 * count], NT)

    diag_ref[...] = folded(diag, core)
    for copy in side_copies:
        copy.wait()


def own_part(place, own, mine, theirs):
    vmem, hbm = pl.BlockSpec(memory_space=pltpu.VMEM), pl.BlockSpec(memory_space=pl.ANY)
    return pl.pallas_call(
        own_kernel,
        in_specs=[pl.BlockSpec(memory_space=pltpu.SMEM), hbm] + [vmem] * 8,
        out_specs=[hbm, vmem],
        scratch_shapes=[
            pltpu.VMEM((4, 20, 4 * ROWS, 640), jnp.bfloat16),
            pltpu.VMEM((6, 1280, 1280), jnp.bfloat16),
            pltpu.VMEM((2, 640, 640), jnp.bfloat16),
            pltpu.VMEM((640, 1280), jnp.bfloat16),
            pltpu.SemaphoreType.DMA((4,)),
            pltpu.SemaphoreType.DMA((4,)),
        ],
        out_shape=[
            jax.ShapeDtypeStruct((4, 1280, 1280), jnp.bfloat16),
            jax.ShapeDtypeStruct((20, 40), jnp.float32),
        ],
        compiler_params=pltpu.CompilerParams(vmem_limit_bytes=44 << 20),
        cost_estimate=FREE,
        name="own_part",
    )(place, own, *mine, *theirs)


def edge_kernel(place_ref, *refs):
    there_refs, (sides_ref, here_ref, back_ref, total) = refs[:-4], refs[-4:]
    step, core = pl.program_id(0), place_ref[0]
    there = [r[...].reshape(320, 640) for r in there_refs[:2]]
    none = jnp.zeros_like(there[0])
    if len(there_refs) == 3:
        there[0] = jnp.where(step == 3, none, there[0])
        there[1] = jnp.where(step == 3, there_refs[2][...].reshape(320, 640), there[1])
    else:
        there[1] = jnp.where(jnp.logical_and(step == 3, core == 0), none, there[1])
    product = dot(side_by_side(there), sides_ref[0], NT)

    @pl.when(step == 0)
    def _():
        total[...] = product

    @pl.when(jnp.logical_and(step > 0, step < 3))
    def _():
        total[...] += product

    @pl.when(step == 3)
    def _():
        tile = folded(total[...] + product, core)
        here_ref[...] = tile[:, :40]
        back_ref[...] = tile[:, 40:]


def edge_part(place, there, sides):
    def rows(at):
        return pl.BlockSpec((20, ROWS, 640), lambda g, p: (0, at(g, p), 0))

    if len(there) == 1:
        specs = [rows(lambda g, p, k=k: 7 * p[0] + 2 * g + k) for k in range(2)]
    else:
        specs = [rows(lambda g, p, k=k: jnp.minimum(2 * g + k, 5)) for k in range(2)] + [rows(lambda g, p: 0)]
    return pl.pallas_call(
        edge_kernel,
        grid_spec=pltpu.PrefetchScalarGridSpec(
            num_scalar_prefetch=1,
            grid=(4,),
            in_specs=specs + [pl.BlockSpec((1, 1280, 1280), lambda g, p: (g, 0, 0))],
            out_specs=[pl.BlockSpec((20, 40), lambda g, p: (0, 0))] * 2,
            scratch_shapes=[pltpu.VMEM((320, 1280), jnp.float32)],
        ),
        out_shape=[jax.ShapeDtypeStruct((20, 40), jnp.float32)] * 2,
        compiler_params=pltpu.CompilerParams(vmem_limit_bytes=24 << 20),
        cost_estimate=FREE,
        name="edge_part",
    )(place, *[there[0]] * 2, *there[1:], sides)


def last_kernel(place_ref, here_ref, back_ref, diag_ref, near_ref, from_near_ref, rest_ref, side_ref, mine_ref, there_ref):
    tile = folded(dot(rest_ref[...].reshape(320, 640), side_ref[0], NT), place_ref[0])
    mine_ref[0] = here_ref[...] + tile[:, :40]
    mine_ref[1] = diag_ref[...]
    mine_ref[2] = near_ref[...]
    mine_ref[3] = from_near_ref[...]
    there_ref[...] = back_ref[...] + tile[:, 40:]


def last_part(place, small, rest, sides):
    def whole(*shape):
        return pl.BlockSpec(shape, lambda g: (0,) * len(shape))

    return pl.pallas_call(
        last_kernel,
        grid=(1,),
        in_specs=[pl.BlockSpec(memory_space=pltpu.SMEM)]
        + [whole(20, 40)] * len(small)
        + [whole(20, ROWS, 640), pl.BlockSpec((1, 1280, 640), lambda g: (3, 0, 0))],
        out_specs=[whole(4, 20, 40), whole(20, 40)],
        out_shape=[jax.ShapeDtypeStruct(shape, jnp.float32) for shape in ((4, 20, 40), (20, 40))],
        compiler_params=pltpu.CompilerParams(vmem_limit_bytes=16 << 20),
        cost_estimate=FREE,
        name="last_part",
    )(place, *small, rest, sides)


def flipped(tile):
    return tile.reshape(20, 2, 20).transpose(2, 1, 0).reshape(20, 40)


def body(factors, lambda_pairs):
    virt, aux = lax.axis_index("virt"), lax.axis_index("aux")
    core = virt % 2
    place = jnp.stack([core, aux // 4, aux % 4]).astype(jnp.int32)
    own = factors.transpose(1, 0, 2)
    half, beside = beside_lambda(lambda_pairs, core)

    def part(first, blocks):
        return lax.dynamic_slice_in_dim(own, ((1 - core) * 7 + first) * ROWS, blocks * ROWS, 1)

    most = part(0, 6)
    beside, most = lax.optimization_barrier((beside, most))
    most = send(most, FAR)
    both = jnp.stack([half, beside])
    ring = [both] + [send(both, route(lambda x, y, z, c, k=k: (x, y - k, z, c))) for k in (1, 2, 3)]
    ring, last, rest = lax.optimization_barrier((ring, own[:, 14 * ROWS :], part(6, 1)))
    last, rest = send(last, from_even(FAR)), send(rest, FAR)

    def before_far(own, *mine):
        theirs = [send(m, NEAR) for m in mine[:2]]
        theirs, *after = lax.optimization_barrier((theirs, *mine[2:]))
        theirs, near = lax.optimization_barrier((theirs + [send(m, NEAR) for m in after], own))
        near = send(near, NEAR)
        sides, diag = own_part(place, own, mine, theirs)
        here, there = edge_part(place, [near], sides)
        return sides, diag, here, send(there, NEAR)

    sides, diag, near_tile, from_near = early(before_far, virt, own, *ring)
    here, back = edge_part(place, [most, last], sides)
    mine, there = last_part(place, [here, back, diag, near_tile, from_near], rest, sides)
    beside_of = lambda pairs: [(s, t ^ 4) for s, t in pairs]
    from_far = send(there, FAR) + send(there, beside_of(FAR))
    total = jnp.concatenate([mine + send(mine, beside_of(HERE)), from_far[None]])
    total = total + sum(lax.ppermute(total, "aux", [(a, a ^ k) for a in range(8)]) for k in (1, 2, 3))
    far_tile, diag, near_tile = flipped(total[0]) + total[4], total[1], flipped(total[2]) + total[3]
    far_tile, diag, near_tile = [t.reshape(20, 2, 20) for t in (far_tile, diag, near_tile)]
    before = jnp.where(core == 0, far_tile, near_tile)
    after = jnp.where(core == 0, near_tile, far_tile)
    return jnp.stack([before, diag, after], 2).transpose(1, 0, 2, 3)


def early(part, virt, *operands):
    def nothing(*operands):
        shapes = jax.eval_shape(part, *operands)
        return jax.tree.map(lambda s: jnp.zeros(s.shape, s.dtype), shapes)

    return lax.cond(virt < lax.axis_size("virt"), part, nothing, *operands)


def solution(mesh):
    placed = (P("aux", "virt", None), P(None, "aux", None))
    return jax.shard_map(
        body, mesh=mesh, in_specs=placed, out_specs=P(None, "virt", None, None), check_vma=False
    )
```

```python
import functools

import jax
import jax.numpy as jnp
from jax import lax
from jax.experimental import pallas as pl
from jax.experimental.pallas import tpu as pltpu
from jax.sharding import PartitionSpec as P

AXES = ("virt", "aux")
ROWS = 16
ORDER = ((0, 1, 2, 3), (0, 1, 3, 2), (0, 1, 2, 3), (0, 1, 2))
FREE = pl.CostEstimate(flops=1, bytes_accessed=1, transcendentals=0)
NT = (((1,), (1,)), ((), ()))
NN = (((1,), (0,)), ((), ()))


def index_of(x, y, z, core):
    return ((z % 8 * 2 + x % 4 // 2) * 2 + core) * 8 + x % 2 * 4 + y % 4


def place_of(index):
    virt, aux = divmod(index, 8)
    return virt // 2 % 2 * 2 + aux // 4, aux % 4, virt // 4, virt % 2


def route(target):
    return [(i, index_of(*target(*place_of(i)))) for i in range(256)]


def from_even(pairs):
    return [(s, t) for s, t in pairs if s // 8 % 2 == 0]


def other_core(x, y, z, core):
    return x, y, z, 1 - core


def across(x, y, z, core):
    step = 1 if core else -1
    chip = z * 2 + x // 2 + step
    return chip % 2 * 2 + x % 2, y, chip // 2 % 8, 1 - core


NEAR, FAR, HERE = route(other_core), route(across), [(i, i) for i in range(256)]


def send(array, pairs):
    return lax.ppermute(array, AXES, pairs)


def beside_lambda(own, core):
    half = lax.dynamic_index_in_dim(own, core, 0, keepdims=False)
    return half, send(half, route(lambda x, y, z, c: (x ^ (3 if c else 1), y, z, c)))


def dot(left, right, dims):
    return lax.dot_general(left, right, dims, preferred_element_type=jnp.float32)


def folded(total, core):
    wide = total.shape[1]
    columns = wide // ROWS
    row = lax.broadcasted_iota(jnp.int32, (ROWS, wide), 0)
    column = lax.broadcasted_iota(jnp.int32, (ROWS, wide), 1) % ROWS
    kept = jnp.where((row == column)[None], total.reshape(-1, ROWS, wide), 0.0).sum(1)
    group = lax.broadcasted_iota(jnp.int32, (wide, columns), 0) // ROWS
    place = group // 40 * 40 + (group + 20 * core) % 40
    ones = (place == lax.broadcasted_iota(jnp.int32, (wide, columns), 1)).astype(jnp.float32)
    return lax.dot_general(
        kept, ones, NN, precision=lax.Precision.HIGHEST, preferred_element_type=jnp.float32
    )


def side_by_side(parts):
    return jnp.concatenate(parts, 1)


def block(array, g):
    return array[:, g * ROWS : (g + 1) * ROWS].reshape(320, -1)


def own_kernel(place_ref, f_hbm, *refs):
    lam_refs, (sides, diag_ref, f_buf, z_buf, rows_cd, cols_cd, f_sem) = refs[:8], refs[8:]
    core = place_ref[0]
    firsts = (7 * core, 7 * core + 4, 8 * (1 - core), 8 * (1 - core) + 4)

    def copied(step):
        count = len(ORDER[step]) * ROWS
        rows = pl.ds(pl.multiple_of(firsts[step] * ROWS, ROWS), count)
        return pltpu.make_async_copy(
            f_hbm.at[:, rows, :], f_buf.at[step, :, pl.ds(0, count), :], f_sem.at[step]
        )

    f_copies = [copied(step) for step in range(4)]
    for copy in f_copies:
        copy.start()

    for k in range(8):
        x_lo, y_at = place_ref[1] ^ (k % 2), (place_ref[2] + k // 2) % 4
        at = pl.ds(pl.multiple_of((x_lo * 4 + y_at) * 80, ROWS), 80)
        for n in range(2):
            part = lam_refs[4 * n + k // 2][k % 2]
            rows_cd[n, at] = part
            cols_cd[at, 640 * n : 640 * n + 640] = part

    diag = 0.0
    for step, order in enumerate(ORDER):
        f_copies[step].wait()
        size = len(order)
        group = f_buf[step, :, : size * ROWS]
        rows = group.reshape(20 * size * ROWS, 640)

        def keep(product, to):
            product = product.astype(jnp.bfloat16).reshape(20, size * ROWS, 1280)
            for n in range(2):
                for k, g in enumerate(order):
                    part = product[:, g * ROWS : (g + 1) * ROWS, 640 * n : 640 * n + 640].reshape(320, 640)
                    to[320 * n : 320 * n + 320, 640 * k : 640 * k + 640] = part

        z = sides.at[step, pl.ds(640, 640)] if step < 2 else z_buf
        keep(dot(rows, rows_cd[...].reshape(1280, 640), NT), z)
        if step < 2:
            keep(dot(rows, cols_cd[...], NN), sides.at[step, pl.ds(0, 640)])
        own = side_by_side([block(group, g) for g in order])
        diag = diag + dot(own, z[:, : 640 * size], NT)

    diag_ref[...] = folded(diag, core)


def in_vmem(array):
    return pltpu.with_memory_space_constraint(array, pltpu.VMEM)


def own_part(place, own, mine, theirs):
    vmem, hbm = pl.BlockSpec(memory_space=pltpu.VMEM), pl.BlockSpec(memory_space=pl.ANY)
    return pl.pallas_call(
        own_kernel,
        in_specs=[pl.BlockSpec(memory_space=pltpu.SMEM), hbm] + [vmem] * 8,
        out_specs=[vmem, vmem],
        scratch_shapes=[
            pltpu.VMEM((4, 20, 4 * ROWS, 640), jnp.bfloat16),
            pltpu.VMEM((640, 2560), jnp.bfloat16),
            pltpu.VMEM((2, 640, 640), jnp.bfloat16),
            pltpu.VMEM((640, 1280), jnp.bfloat16),
            pltpu.SemaphoreType.DMA((4,)),
        ],
        out_shape=[
            pltpu.VMEM((2, 1280, 2560), jnp.bfloat16),
            jax.ShapeDtypeStruct((20, 40), jnp.float32),
        ],
        compiler_params=pltpu.CompilerParams(vmem_limit_bytes=36 << 20),
        cost_estimate=FREE,
        name="own_part",
    )(place, own, *mine, *theirs)


def edge_kernel(near, place_ref, *refs):
    *there_refs, sides_ref, here_ref, back_ref, buf, sem = refs[: 7 - near]
    core = place_ref[0]

    def copied(source, row, at):
        rows = pl.ds(pl.multiple_of(row * ROWS, ROWS), ROWS)
        return pltpu.make_async_copy(
            source.at[:, rows, :], buf.at[at // 4, :, :, pl.ds(640 * (at % 4), 640)], sem.at[at]
        )

    if near:
        copies = [copied(there_refs[0], 7 * core + k, at) for at, k in enumerate((0, 1, 2, 3, 4, 5, 7, 6))]
    else:
        copies = [copied(there_refs[0], at, at) for at in range(6)] + [copied(there_refs[1], 0, 6)]
    sides = sides_ref
    if not near:
        sides, sides_sem = refs[7:]
        halves = [pltpu.make_async_copy(sides_ref.at[i], sides.at[i], sides_sem.at[i]) for i in range(2)]
        copies = copies[:4] + halves[:1] + copies[4:] + halves[1:]
    for copy in copies:
        copy.start()
    first = 4 if near else 5
    for copy in copies[:first]:
        copy.wait()
    total = dot(buf[0].reshape(320, 2560), sides[0], NT)
    for copy in copies[first:]:
        copy.wait()
    if near:

        @pl.when(core == 0)
        def _():
            buf[1, :, :, 1280:1920] = jnp.zeros((20, ROWS, 640), jnp.bfloat16)

    wide = 2560 if near else 1920
    total = total + dot(buf[1, :, :, :wide].reshape(320, wide), sides[1, :, :wide], NT)
    tile = folded(total, core)
    here_ref[...] = tile[:, :40]
    back_ref[...] = tile[:, 40:]


def edge_part(place, there, sides):
    vmem, hbm = pl.BlockSpec(memory_space=pltpu.VMEM), pl.BlockSpec(memory_space=pl.ANY)
    near = len(there) == 1
    held = [] if near else [pltpu.VMEM((2, 1280, 2560), jnp.bfloat16), pltpu.SemaphoreType.DMA((2,))]
    return pl.pallas_call(
        functools.partial(edge_kernel, near),
        in_specs=[pl.BlockSpec(memory_space=pltpu.SMEM)] + [hbm] * len(there) + [vmem if near else hbm],
        out_specs=[vmem, vmem],
        scratch_shapes=[pltpu.VMEM((2, 20, ROWS, 2560), jnp.bfloat16), pltpu.SemaphoreType.DMA((8,))] + held,
        out_shape=[jax.ShapeDtypeStruct((20, 40), jnp.float32)] * 2,
        compiler_params=pltpu.CompilerParams(vmem_limit_bytes=(24 if near else 40) << 20),
        cost_estimate=FREE,
        name="edge_part",
    )(place, *there, in_vmem(sides) if near else sides)


def last_kernel(place_ref, here_ref, back_ref, diag_ref, near_ref, from_near_ref, rest_ref, side_ref, mine_ref, there_ref):
    tile = folded(dot(rest_ref[...].reshape(320, 640), side_ref[0], NT), place_ref[0])
    mine_ref[:, :40] = here_ref[...] + tile[:, :40]
    mine_ref[:, 40:80] = diag_ref[...]
    mine_ref[:, 80:120] = near_ref[...]
    mine_ref[:, 120:160] = from_near_ref[...]
    there_ref[...] = back_ref[...] + tile[:, 40:]


def last_part(place, small, rest, sides):
    def whole(*shape):
        return pl.BlockSpec(shape, lambda g: (0,) * len(shape))

    return pl.pallas_call(
        last_kernel,
        grid=(1,),
        in_specs=[pl.BlockSpec(memory_space=pltpu.SMEM)]
        + [whole(20, 40)] * len(small)
        + [whole(20, ROWS, 640), pl.BlockSpec((1, 1280, 640), lambda g: (1, 0, 3))],
        out_specs=[whole(20, 160), whole(20, 40)],
        out_shape=[jax.ShapeDtypeStruct(shape, jnp.float32) for shape in ((20, 160), (20, 40))],
        compiler_params=pltpu.CompilerParams(vmem_limit_bytes=16 << 20),
        cost_estimate=FREE,
        name="last_part",
    )(place, *small, rest, sides)


def flipped(tile):
    return tile.reshape(20, 2, 20).transpose(2, 1, 0).reshape(20, 40)


def body(factors, lambda_pairs):
    virt, aux = lax.axis_index("virt"), lax.axis_index("aux")
    core = virt % 2
    place = jnp.stack([core, aux // 4, aux % 4]).astype(jnp.int32)
    own = factors.transpose(1, 0, 2)
    half, beside = beside_lambda(lambda_pairs, core)

    def part(first, blocks):
        return lax.dynamic_slice_in_dim(own, ((1 - core) * 7 + first) * ROWS, blocks * ROWS, 1)

    most = part(0, 6)
    beside, most = lax.optimization_barrier((beside, most))
    most = send(most, FAR)
    both = jnp.stack([half, beside])
    ring = [both] + [send(both, route(lambda x, y, z, c, k=k: (x, y - k, z, c))) for k in (1, 2, 3)]
    ring, last, rest = lax.optimization_barrier((ring, own[:, 14 * ROWS :], part(6, 1)))
    last, rest = send(last, from_even(FAR)), send(rest, FAR)

    def before_far(own, *mine):
        theirs = [send(m, NEAR) for m in mine[:2]]
        theirs, *after = lax.optimization_barrier((theirs, *mine[2:]))
        theirs, near = lax.optimization_barrier((theirs + [send(m, NEAR) for m in after], own))
        near = send(near, NEAR)
        sides, diag = own_part(place, own, mine, theirs)
        here, there = edge_part(place, [near], sides)
        return sides, diag, here, send(there, NEAR)

    sides, diag, near_tile, from_near = early(before_far, virt, own, *ring)
    here, back = edge_part(place, [most, last], sides)
    mine, there = last_part(place, [here, back, diag, near_tile, from_near], rest, sides)
    beside_of = lambda pairs: [(s, t ^ 4) for s, t in pairs]
    from_far = send(there, FAR) + send(there, beside_of(FAR))
    total = jnp.concatenate([mine + send(mine, beside_of(HERE)), from_far], 1)
    total = total + sum(lax.ppermute(total, "aux", [(a, a ^ k) for a in range(8)]) for k in (1, 2, 3))
    far_tile, diag, near_tile, from_near, from_far = [total[:, i : i + 40] for i in range(0, 200, 40)]
    far_tile, near_tile = flipped(far_tile) + from_far, flipped(near_tile) + from_near
    far_tile, diag, near_tile = [t.reshape(20, 2, 20) for t in (far_tile, diag, near_tile)]
    before = jnp.where(core == 0, far_tile, near_tile)
    after = jnp.where(core == 0, near_tile, far_tile)
    return jnp.stack([before, diag, after], 1).transpose(2, 0, 1, 3)


def early(part, virt, *operands):
    def nothing(*operands):
        shapes = jax.eval_shape(part, *operands)
        return jax.tree.map(lambda s: jnp.zeros(s.shape, s.dtype), shapes)

    return lax.cond(virt < lax.axis_size("virt"), part, nothing, *operands)


def solution(mesh):
    placed = (P("aux", "virt", None), P(None, "aux", None))
    return jax.shard_map(
        body, mesh=mesh, in_specs=placed, out_specs=P(None, "virt", None, None), check_vma=False
    )
```

```python
import functools

import jax
import jax.numpy as jnp
from jax import lax
from jax.experimental import pallas as pl
from jax.experimental.pallas import tpu as pltpu
from jax.sharding import PartitionSpec as P

AXES = ("virt", "aux")
ROWS = 16
ORDER = ((0, 1, 2, 3), (0, 3, 1, 2), (0, 1, 2, 3), (0, 1, 2))
FREE = pl.CostEstimate(flops=1, bytes_accessed=1, transcendentals=0)
NT = (((1,), (1,)), ((), ()))
NN = (((1,), (0,)), ((), ()))


def index_of(x, y, z, core):
    return ((z % 8 * 2 + x % 4 // 2) * 2 + core) * 8 + x % 2 * 4 + y % 4


def place_of(index):
    virt, aux = divmod(index, 8)
    return virt // 2 % 2 * 2 + aux // 4, aux % 4, virt // 4, virt % 2


def route(target):
    return [(i, index_of(*target(*place_of(i)))) for i in range(256)]


def from_even(pairs):
    return [(s, t) for s, t in pairs if s // 8 % 2 == 0]


def other_core(x, y, z, core):
    return x, y, z, 1 - core


def across(x, y, z, core):
    step = 1 if core else -1
    chip = z * 2 + x // 2 + step
    return chip % 2 * 2 + x % 2, y, chip // 2 % 8, 1 - core


NEAR, FAR, HERE = route(other_core), route(across), [(i, i) for i in range(256)]


def send(array, pairs):
    return lax.ppermute(array, AXES, pairs)


def beside_lambda(own, core):
    half = lax.dynamic_index_in_dim(own, core, 0, keepdims=False)
    return half, send(half, route(lambda x, y, z, c: (x ^ (3 if c else 1), y, z, c)))


def dot(left, right, dims):
    return lax.dot_general(left, right, dims, preferred_element_type=jnp.float32)


def folded(total, core):
    wide = total.shape[1]
    columns = wide // ROWS
    row = lax.broadcasted_iota(jnp.int32, (ROWS, wide), 0)
    column = lax.broadcasted_iota(jnp.int32, (ROWS, wide), 1) % ROWS
    kept = jnp.where((row == column)[None], total.reshape(-1, ROWS, wide), 0.0).sum(1)
    group = lax.broadcasted_iota(jnp.int32, (wide, columns), 0) // ROWS
    place = group // 40 * 40 + (group + 20 * core) % 40
    ones = (place == lax.broadcasted_iota(jnp.int32, (wide, columns), 1)).astype(jnp.float32)
    return lax.dot_general(
        kept, ones, NN, precision=lax.Precision.HIGHEST, preferred_element_type=jnp.float32
    )


def side_by_side(parts):
    return jnp.concatenate(parts, 1)


def block(array, g):
    return array[:, g * ROWS : (g + 1) * ROWS].reshape(320, -1)


def own_kernel(place_ref, f_hbm, *refs):
    lam_refs, (sides, diag_ref, f_buf, z_buf, rows_cd, cols_cd, f_sem) = refs[:8], refs[8:]
    core = place_ref[0]
    firsts = (7 * core, 7 * core + 4, 8 * (1 - core), 8 * (1 - core) + 4)

    def copied(step):
        count = len(ORDER[step]) * ROWS
        rows = pl.ds(pl.multiple_of(firsts[step] * ROWS, ROWS), count)
        return pltpu.make_async_copy(
            f_hbm.at[:, rows, :], f_buf.at[step, :, pl.ds(0, count), :], f_sem.at[step]
        )

    f_copies = [copied(step) for step in range(4)]
    for copy in f_copies:
        copy.start()

    for k in range(8):
        x_lo, y_at = place_ref[1] ^ (k % 2), (place_ref[2] + k // 2) % 4
        at = pl.ds(pl.multiple_of((x_lo * 4 + y_at) * 80, ROWS), 80)
        for n in range(2):
            part = lam_refs[4 * n + k // 2][k % 2]
            rows_cd[n, at] = part
            cols_cd[at, 640 * n : 640 * n + 640] = part

    diag = 0.0
    for step, order in enumerate(ORDER):
        f_copies[step].wait()
        size = len(order)
        group = f_buf[step, :, : size * ROWS]
        rows = group.reshape(20 * size * ROWS, 640)

        def keep(product, to):
            product = product.astype(jnp.bfloat16).reshape(20, size * ROWS, 1280)
            for n in range(2):
                for k, g in enumerate(order):
                    part = product[:, g * ROWS : (g + 1) * ROWS, 640 * n : 640 * n + 640].reshape(320, 640)
                    to[320 * n : 320 * n + 320, 640 * k : 640 * k + 640] = part

        z = sides.at[step, pl.ds(640, 640)] if step < 2 else z_buf
        keep(dot(rows, rows_cd[...].reshape(1280, 640), NT), z)
        if step < 2:
            keep(dot(rows, cols_cd[...], NN), sides.at[step, pl.ds(0, 640)])
        own = side_by_side([block(group, g) for g in order])
        diag = diag + dot(own, z[:, : 640 * size], NT)

    diag_ref[...] = folded(diag, core)


def in_vmem(array):
    return pltpu.with_memory_space_constraint(array, pltpu.VMEM)


def own_part(place, own, mine, theirs):
    vmem, hbm = pl.BlockSpec(memory_space=pltpu.VMEM), pl.BlockSpec(memory_space=pl.ANY)
    return pl.pallas_call(
        own_kernel,
        in_specs=[pl.BlockSpec(memory_space=pltpu.SMEM), hbm] + [vmem] * 8,
        out_specs=[vmem, vmem],
        scratch_shapes=[
            pltpu.VMEM((4, 20, 4 * ROWS, 640), jnp.bfloat16),
            pltpu.VMEM((640, 2560), jnp.bfloat16),
            pltpu.VMEM((2, 640, 640), jnp.bfloat16),
            pltpu.VMEM((640, 1280), jnp.bfloat16),
            pltpu.SemaphoreType.DMA((4,)),
        ],
        out_shape=[
            pltpu.VMEM((2, 1280, 2560), jnp.bfloat16),
            jax.ShapeDtypeStruct((20, 40), jnp.float32),
        ],
        compiler_params=pltpu.CompilerParams(vmem_limit_bytes=36 << 20),
        cost_estimate=FREE,
        name="own_part",
    )(place, own, *mine, *theirs)


def edge_kernel(near, place_ref, *refs):
    *there_refs, sides_ref, here_ref, back_ref, buf, sem = refs[: 7 - near]
    core = place_ref[0]

    def copied(source, row, at):
        rows = pl.ds(pl.multiple_of(row * ROWS, ROWS), ROWS)
        return pltpu.make_async_copy(
            source.at[:, rows, :], buf.at[at // 4, :, :, pl.ds(640 * (at % 4), 640)], sem.at[at]
        )

    if near:
        copies = [copied(there_refs[0], 7 * core + k, at) for at, k in enumerate((0, 1, 2, 3, 4, 7, 5, 6))]
    else:
        copies = [copied(there_refs[0], at, at) for at in range(5)] + [copied(there_refs[1], 0, 5)]
    sides = sides_ref
    if not near:
        sides, sides_sem = refs[7:]
        halves = [
            pltpu.make_async_copy(sides_ref.at[i, :, columns], sides.at[i, :, columns], sides_sem.at[i])
            for i, columns in enumerate((pl.ds(0, 2560), pl.ds(0, 1280)))
        ]
        copies = copies[:4] + halves[:1] + copies[4:] + halves[1:]
    for copy in copies:
        copy.start()
    first = 4 if near else 5
    for copy in copies[:first]:
        copy.wait()
    total = dot(buf[0].reshape(320, 2560), sides[0], NT)
    for copy in copies[first:]:
        copy.wait()
    if near:

        @pl.when(core == 0)
        def _():
            buf[1, :, :, 640:1280] = jnp.zeros((20, ROWS, 640), jnp.bfloat16)

    wide = 2560 if near else 1280
    total = total + dot(buf[1, :, :, :wide].reshape(320, wide), sides[1, :, :wide], NT)
    tile = folded(total, core)
    here_ref[...] = tile[:, :40]
    back_ref[...] = tile[:, 40:]


def edge_part(place, there, sides):
    vmem, hbm = pl.BlockSpec(memory_space=pltpu.VMEM), pl.BlockSpec(memory_space=pl.ANY)
    near = len(there) == 1
    held = [] if near else [pltpu.VMEM((2, 1280, 2560), jnp.bfloat16), pltpu.SemaphoreType.DMA((2,))]
    return pl.pallas_call(
        functools.partial(edge_kernel, near),
        in_specs=[pl.BlockSpec(memory_space=pltpu.SMEM)] + [hbm] * len(there) + [vmem if near else hbm],
        out_specs=[vmem, vmem],
        scratch_shapes=[pltpu.VMEM((2, 20, ROWS, 2560), jnp.bfloat16), pltpu.SemaphoreType.DMA((8,))] + held,
        out_shape=[jax.ShapeDtypeStruct((20, 40), jnp.float32)] * 2,
        compiler_params=pltpu.CompilerParams(vmem_limit_bytes=(24 if near else 40) << 20),
        cost_estimate=FREE,
        name="edge_part",
    )(place, *there, in_vmem(sides) if near else sides)


def last_kernel(place_ref, here_ref, back_ref, diag_ref, near_ref, from_near_ref, rest_ref, side_ref, mine_ref, there_ref):
    rest = side_by_side([block(rest_ref, 0), block(rest_ref, 1)])
    tile = folded(dot(rest, side_ref[0], NT), place_ref[0])
    mine_ref[:, :40] = here_ref[...] + tile[:, :40]
    mine_ref[:, 40:80] = diag_ref[...]
    mine_ref[:, 80:120] = near_ref[...]
    mine_ref[:, 120:160] = from_near_ref[...]
    there_ref[...] = back_ref[...] + tile[:, 40:]


def last_part(place, small, rest, sides):
    def whole(*shape):
        return pl.BlockSpec(shape, lambda g: (0,) * len(shape))

    return pl.pallas_call(
        last_kernel,
        grid=(1,),
        in_specs=[pl.BlockSpec(memory_space=pltpu.SMEM)]
        + [whole(20, 40)] * len(small)
        + [whole(20, 2 * ROWS, 640), pl.BlockSpec((1, 1280, 1280), lambda g: (1, 0, 1))],
        out_specs=[whole(20, 160), whole(20, 40)],
        out_shape=[jax.ShapeDtypeStruct(shape, jnp.float32) for shape in ((20, 160), (20, 40))],
        compiler_params=pltpu.CompilerParams(vmem_limit_bytes=16 << 20),
        cost_estimate=FREE,
        name="last_part",
    )(place, *small, rest, sides)


def flipped(tile):
    return tile.reshape(20, 2, 20).transpose(2, 1, 0).reshape(20, 40)


def body(factors, lambda_pairs):
    virt, aux = lax.axis_index("virt"), lax.axis_index("aux")
    core = virt % 2
    place = jnp.stack([core, aux // 4, aux % 4]).astype(jnp.int32)
    own = factors.transpose(1, 0, 2)
    half, beside = beside_lambda(lambda_pairs, core)

    def part(first, blocks):
        return lax.dynamic_slice_in_dim(own, ((1 - core) * 7 + first) * ROWS, blocks * ROWS, 1)

    most = part(0, 5)
    beside, most = lax.optimization_barrier((beside, most))
    most = send(most, FAR)
    both = jnp.stack([half, beside])
    ring = [both] + [send(both, route(lambda x, y, z, c, k=k: (x, y - k, z, c))) for k in (1, 2, 3)]
    ring, last, rest = lax.optimization_barrier((ring, own[:, 14 * ROWS :], part(5, 2)))
    last, rest = send(last, from_even(FAR)), send(rest, FAR)

    def before_far(own, *mine):
        theirs = [send(m, NEAR) for m in mine[:2]]
        theirs, *after = lax.optimization_barrier((theirs, *mine[2:]))
        theirs, near = lax.optimization_barrier((theirs + [send(m, NEAR) for m in after], own))
        near = send(near, NEAR)
        sides, diag = own_part(place, own, mine, theirs)
        here, there = edge_part(place, [near], sides)
        return sides, diag, here, send(there, NEAR)

    sides, diag, near_tile, from_near = early(before_far, virt, own, *ring)
    here, back = edge_part(place, [most, last], sides)
    mine, there = last_part(place, [here, back, diag, near_tile, from_near], rest, sides)
    beside_of = lambda pairs: [(s, t ^ 4) for s, t in pairs]
    from_far = send(there, FAR) + send(there, beside_of(FAR))
    total = jnp.concatenate([mine + send(mine, beside_of(HERE)), from_far], 1)
    total = total + sum(lax.ppermute(total, "aux", [(a, a ^ k) for a in range(8)]) for k in (1, 2, 3))
    far_tile, diag, near_tile, from_near, from_far = [total[:, i : i + 40] for i in range(0, 200, 40)]
    far_tile, near_tile = flipped(far_tile) + from_far, flipped(near_tile) + from_near
    far_tile, diag, near_tile = [t.reshape(20, 2, 20) for t in (far_tile, diag, near_tile)]
    before = jnp.where(core == 0, far_tile, near_tile)
    after = jnp.where(core == 0, near_tile, far_tile)
    return jnp.stack([before, diag, after], 1).transpose(2, 0, 1, 3)


def early(part, virt, *operands):
    def nothing(*operands):
        shapes = jax.eval_shape(part, *operands)
        return jax.tree.map(lambda s: jnp.zeros(s.shape, s.dtype), shapes)

    return lax.cond(virt < lax.axis_size("virt"), part, nothing, *operands)


def solution(mesh):
    placed = (P("aux", "virt", None), P(None, "aux", None))
    return jax.shard_map(
        body, mesh=mesh, in_specs=placed, out_specs=P(None, "virt", None, None), check_vma=False
    )
```

```python
import functools

import jax
import jax.numpy as jnp
from jax import lax
from jax.experimental import pallas as pl
from jax.experimental.pallas import tpu as pltpu
from jax.sharding import PartitionSpec as P

AXES = ("virt", "aux")
ROWS = 16
ORDER = ((0, 1, 2, 3), (1, 2, 3, 0), (0, 1, 2, 3), (0, 1, 2))
FREE = pl.CostEstimate(flops=1, bytes_accessed=1, transcendentals=0)
NT = (((1,), (1,)), ((), ()))
NN = (((1,), (0,)), ((), ()))


def index_of(x, y, z, core):
    return ((z % 8 * 2 + x % 4 // 2) * 2 + core) * 8 + x % 2 * 4 + y % 4


def place_of(index):
    virt, aux = divmod(index, 8)
    return virt // 2 % 2 * 2 + aux // 4, aux % 4, virt // 4, virt % 2


def route(target):
    return [(i, index_of(*target(*place_of(i)))) for i in range(256)]


def from_even(pairs):
    return [(s, t) for s, t in pairs if s // 8 % 2 == 0]


def other_core(x, y, z, core):
    return x, y, z, 1 - core


def across(x, y, z, core):
    step = 1 if core else -1
    chip = z * 2 + x // 2 + step
    return chip % 2 * 2 + x % 2, y, chip // 2 % 8, 1 - core


NEAR, FAR, HERE = route(other_core), route(across), [(i, i) for i in range(256)]


def send(array, pairs):
    return lax.ppermute(array, AXES, pairs)


def beside_lambda(own, core):
    half = lax.dynamic_index_in_dim(own, core, 0, keepdims=False)
    return half, send(half, route(lambda x, y, z, c: (x ^ (3 if c else 1), y, z, c)))


def dot(left, right, dims):
    return lax.dot_general(left, right, dims, preferred_element_type=jnp.float32)


def folded(total, core):
    wide = total.shape[1]
    columns = wide // ROWS
    row = lax.broadcasted_iota(jnp.int32, (ROWS, wide), 0)
    column = lax.broadcasted_iota(jnp.int32, (ROWS, wide), 1) % ROWS
    kept = jnp.where((row == column)[None], total.reshape(-1, ROWS, wide), 0.0).sum(1)
    group = lax.broadcasted_iota(jnp.int32, (wide, columns), 0) // ROWS
    place = group // 40 * 40 + (group + 20 * core) % 40
    ones = (place == lax.broadcasted_iota(jnp.int32, (wide, columns), 1)).astype(jnp.float32)
    return lax.dot_general(
        kept, ones, NN, precision=lax.Precision.HIGHEST, preferred_element_type=jnp.float32
    )


def side_by_side(parts):
    return jnp.concatenate(parts, 1)


def block(array, g):
    return array[:, g * ROWS : (g + 1) * ROWS].reshape(320, -1)


def own_kernel(place_ref, f_hbm, *refs):
    lam_refs, (sides, diag_ref, f_buf, z_buf, rows_cd, cols_cd, f_sem) = refs[:8], refs[8:]
    core = place_ref[0]
    firsts = (7 * core, 7 * core + 4, 8 * (1 - core), 8 * (1 - core) + 4)

    def copied(step):
        count = len(ORDER[step]) * ROWS
        rows = pl.ds(pl.multiple_of(firsts[step] * ROWS, ROWS), count)
        return pltpu.make_async_copy(
            f_hbm.at[:, rows, :], f_buf.at[step, :, pl.ds(0, count), :], f_sem.at[step]
        )

    f_copies = [copied(step) for step in range(4)]
    for copy in f_copies:
        copy.start()

    for k in range(8):
        x_lo, y_at = place_ref[1] ^ (k % 2), (place_ref[2] + k // 2) % 4
        at = pl.ds(pl.multiple_of((x_lo * 4 + y_at) * 80, ROWS), 80)
        for n in range(2):
            part = lam_refs[4 * n + k // 2][k % 2]
            rows_cd[n, at] = part
            cols_cd[at, 640 * n : 640 * n + 640] = part

    diag = 0.0
    for step, order in enumerate(ORDER):
        f_copies[step].wait()
        size = len(order)
        group = f_buf[step, :, : size * ROWS]
        rows = group.reshape(20 * size * ROWS, 640)

        def keep(product, to):
            product = product.astype(jnp.bfloat16).reshape(20, size * ROWS, 1280)
            for n in range(2):
                for k, g in enumerate(order):
                    part = product[:, g * ROWS : (g + 1) * ROWS, 640 * n : 640 * n + 640].reshape(320, 640)
                    to[320 * n : 320 * n + 320, 640 * k : 640 * k + 640] = part

        z = sides.at[step, pl.ds(640, 640)] if step < 2 else z_buf
        keep(dot(rows, rows_cd[...].reshape(1280, 640), NT), z)
        if step < 2:
            keep(dot(rows, cols_cd[...], NN), sides.at[step, pl.ds(0, 640)])
        own = side_by_side([block(group, g) for g in order])
        diag = diag + dot(own, z[:, : 640 * size], NT)

    diag_ref[...] = folded(diag, core)


def in_vmem(array):
    return pltpu.with_memory_space_constraint(array, pltpu.VMEM)


def own_part(place, own, mine, theirs):
    vmem, hbm = pl.BlockSpec(memory_space=pltpu.VMEM), pl.BlockSpec(memory_space=pl.ANY)
    return pl.pallas_call(
        own_kernel,
        in_specs=[pl.BlockSpec(memory_space=pltpu.SMEM), hbm] + [vmem] * 8,
        out_specs=[vmem, vmem],
        scratch_shapes=[
            pltpu.VMEM((4, 20, 4 * ROWS, 640), jnp.bfloat16),
            pltpu.VMEM((640, 2560), jnp.bfloat16),
            pltpu.VMEM((2, 640, 640), jnp.bfloat16),
            pltpu.VMEM((640, 1280), jnp.bfloat16),
            pltpu.SemaphoreType.DMA((4,)),
        ],
        out_shape=[
            pltpu.VMEM((2, 1280, 2560), jnp.bfloat16),
            jax.ShapeDtypeStruct((20, 40), jnp.float32),
        ],
        compiler_params=pltpu.CompilerParams(vmem_limit_bytes=36 << 20),
        cost_estimate=FREE,
        name="own_part",
    )(place, own, *mine, *theirs)


def edge_kernel(near, place_ref, *refs):
    *there_refs, sides_ref, here_ref, back_ref, buf, sem = refs[:6]
    core = place_ref[0]

    def copied(source, row, at):
        rows = pl.ds(pl.multiple_of(row * ROWS, ROWS), ROWS)
        return pltpu.make_async_copy(
            source.at[:, rows, :], buf.at[at // 4, :, :, pl.ds(640 * (at % 4), 640)], sem.at[at]
        )

    if near:
        copies = [copied(there_refs[0], 7 * core + k, at) for at, k in enumerate((0, 1, 2, 3, 5, 6, 7, 4))]
    else:
        copies = [copied(there_refs[0], k, at) for k, at in enumerate((0, 1, 2, 3, 7))]
    sides = sides_ref
    if not near:
        sides, sides_sem = refs[6:]
        halves = [
            pltpu.make_async_copy(sides_ref.at[i, :, columns], sides.at[i, :, columns], sides_sem.at[i])
            for i, columns in enumerate((pl.ds(0, 2560), pl.ds(1920, 640)))
        ]
        copies = copies[:4] + halves[:1] + copies[4:] + halves[1:]
    for copy in copies:
        copy.start()
    first = 4 if near else 5
    for copy in copies[:first]:
        copy.wait()
    total = dot(buf[0].reshape(320, 2560), sides[0], NT)
    for copy in copies[first:]:
        copy.wait()
    if near:

        @pl.when(core == 0)
        def _():
            buf[1, :, :, 1280:1920] = jnp.zeros((20, ROWS, 640), jnp.bfloat16)

    start = 0 if near else 1920
    total = total + dot(buf[1, :, :, start:].reshape(320, 2560 - start), sides[1, :, start:], NT)
    tile = folded(total, core)
    here_ref[...] = tile[:, :40]
    back_ref[...] = tile[:, 40:]


def edge_part(place, there, sides, near):
    vmem, hbm = pl.BlockSpec(memory_space=pltpu.VMEM), pl.BlockSpec(memory_space=pl.ANY)
    held = [] if near else [pltpu.VMEM((2, 1280, 2560), jnp.bfloat16), pltpu.SemaphoreType.DMA((2,))]
    return pl.pallas_call(
        functools.partial(edge_kernel, near),
        in_specs=[pl.BlockSpec(memory_space=pltpu.SMEM)] + [hbm] * len(there) + [vmem if near else hbm],
        out_specs=[vmem, vmem],
        scratch_shapes=[pltpu.VMEM((2, 20, ROWS, 2560), jnp.bfloat16), pltpu.SemaphoreType.DMA((8,))] + held,
        out_shape=[jax.ShapeDtypeStruct((20, 40), jnp.float32)] * 2,
        compiler_params=pltpu.CompilerParams(vmem_limit_bytes=(24 if near else 40) << 20),
        cost_estimate=FREE,
        name="edge_part",
    )(place, *there, in_vmem(sides) if near else sides)


def last_kernel(place_ref, here_ref, back_ref, diag_ref, near_ref, from_near_ref, rest_ref, last_ref, side_ref, mine_ref, there_ref):
    rest = side_by_side([block(rest_ref, 0), block(rest_ref, 1), block(last_ref, 0)])
    tile = folded(dot(rest, side_ref[0], NT), place_ref[0])
    mine_ref[:, :40] = here_ref[...] + tile[:, :40]
    mine_ref[:, 40:80] = diag_ref[...]
    mine_ref[:, 80:120] = near_ref[...]
    mine_ref[:, 120:160] = from_near_ref[...]
    there_ref[...] = back_ref[...] + tile[:, 40:]


def last_part(place, small, rest, last, sides):
    def whole(*shape):
        return pl.BlockSpec(shape, lambda g: (0,) * len(shape))

    return pl.pallas_call(
        last_kernel,
        grid=(1,),
        in_specs=[pl.BlockSpec(memory_space=pltpu.SMEM)]
        + [whole(20, 40)] * len(small)
        + [whole(20, 2 * ROWS, 640), whole(20, ROWS, 640), pl.BlockSpec((1, 1280, 1920), lambda g: (1, 0, 0))],
        out_specs=[whole(20, 160), whole(20, 40)],
        out_shape=[jax.ShapeDtypeStruct(shape, jnp.float32) for shape in ((20, 160), (20, 40))],
        compiler_params=pltpu.CompilerParams(vmem_limit_bytes=24 << 20),
        cost_estimate=FREE,
        name="last_part",
    )(place, *small, rest, last, sides)


def flipped(tile):
    return tile.reshape(20, 2, 20).transpose(2, 1, 0).reshape(20, 40)


def body(factors, lambda_pairs):
    virt, aux = lax.axis_index("virt"), lax.axis_index("aux")
    core = virt % 2
    place = jnp.stack([core, aux // 4, aux % 4]).astype(jnp.int32)
    own = factors.transpose(1, 0, 2)
    half, beside = beside_lambda(lambda_pairs, core)

    def part(first, blocks):
        return lax.dynamic_slice_in_dim(own, ((1 - core) * 7 + first) * ROWS, blocks * ROWS, 1)

    most = part(0, 5)
    beside, most = lax.optimization_barrier((beside, most))
    most = send(most, FAR)
    both = jnp.stack([half, beside])
    ring = [both] + [send(both, route(lambda x, y, z, c, k=k: (x, y - k, z, c))) for k in (1, 2, 3)]
    ring, last, rest = lax.optimization_barrier((ring, own[:, 14 * ROWS :], part(5, 2)))
    last, rest = send(last, from_even(FAR)), send(rest, FAR)

    def before_far(own, *mine):
        theirs = [send(m, NEAR) for m in mine[:2]]
        theirs, *after = lax.optimization_barrier((theirs, *mine[2:]))
        theirs, near = lax.optimization_barrier((theirs + [send(m, NEAR) for m in after], own))
        near = send(near, NEAR)
        sides, diag = own_part(place, own, mine, theirs)
        here, there = edge_part(place, [near], sides, True)
        return sides, diag, here, send(there, NEAR)

    sides, diag, near_tile, from_near = early(before_far, virt, own, *ring)
    here, back = edge_part(place, [most], sides, False)
    mine, there = last_part(place, [here, back, diag, near_tile, from_near], rest, last, sides)
    beside_of = lambda pairs: [(s, t ^ 4) for s, t in pairs]
    from_far = send(there, FAR) + send(there, beside_of(FAR))
    total = jnp.concatenate([mine + send(mine, beside_of(HERE)), from_far], 1)
    total = total + sum(lax.ppermute(total, "aux", [(a, a ^ k) for a in range(8)]) for k in (1, 2, 3))
    far_tile, diag, near_tile, from_near, from_far = [total[:, i : i + 40] for i in range(0, 200, 40)]
    far_tile, near_tile = flipped(far_tile) + from_far, flipped(near_tile) + from_near
    far_tile, diag, near_tile = [t.reshape(20, 2, 20) for t in (far_tile, diag, near_tile)]
    before = jnp.where(core == 0, far_tile, near_tile)
    after = jnp.where(core == 0, near_tile, far_tile)
    return jnp.stack([before, diag, after], 1).transpose(2, 0, 1, 3)


def early(part, virt, *operands):
    def nothing(*operands):
        shapes = jax.eval_shape(part, *operands)
        return jax.tree.map(lambda s: jnp.zeros(s.shape, s.dtype), shapes)

    return lax.cond(virt < lax.axis_size("virt"), part, nothing, *operands)


def solution(mesh):
    placed = (P("aux", "virt", None), P(None, "aux", None))
    return jax.shard_map(
        body, mesh=mesh, in_specs=placed, out_specs=P(None, "virt", None, None), check_vma=False
    )
```
